512 devices in a mesh: row: 8 (over z_lo, core), col: 16 (over y, z_hi), depth: 4 (over x).
Axes of the slice: x: 4, y: 8, z: 8 (z_hi: 2, z_lo: 4; z = z_hi * 4 + z_lo), core: 2. Of those that a mesh axis runs over, the one named last changes fastest.
Arguments:
- adjoint_slab: bfloat16 [12288, 65536], P('row', ('col', 'depth')), may hold values from -16 to 16
- panel_cols: bfloat16 [65536, 512], P(('col', 'depth'), 'row'), may hold values from -0.0234375 to 0.0234375
- incoming: float32 [12288, 512], P(('row', 'col', 'depth')), may hold values from -6 to 6
- inverse_block: float32 [512, 512], replicated, may hold values from -0.2 to 2, as said below
- panel_rows: bfloat16 [12288, 512], P(('row', 'col', 'depth')), may hold values from -0.0546875 to 0.0546875
Outputs:
- grad_rows: float32 [12288, 512], P(('row', 'col', 'depth'))
- panel_term: float32 [512, 512], replicated
The draws below stay inside these ranges and needn't reach their ends.
Inputs may be any that keep to these rules, and one draw needn't show every extreme that they name: inverse_block is lower triangular with diagonal between 1 and 2.
All inputs are finite; a program needn't handle non-finite values.
Results may differ from the reference program's by a relative error of at most 0.0003.
Values may be sent and summed in bfloat16 or wider, within the bound.
A program may use at most 64 MiB of HBM per device.

```python
import jax
import jax.numpy as jnp
from jax import lax

B = 512
M = 65536
ROW_DEV = 1536
ROWS = 12288
N_ROW = 8


def draw_inverse_block(key, part):
    key = jax.random.fold_in(key, 7)
    first_key, second_key = jax.random.split(key)
    lower = jnp.clip(jax.random.normal(first_key, (B, B), jnp.float32), -4.0, 4.0) * (0.5 / jnp.sqrt(B * 1.0))
    middle = jax.random.uniform(second_key, (B,), jnp.float32, 1.0, 2.0)
    lower = jnp.clip(lower, -0.2, 0.2)
    row_ids = lax_iota(B)
    below = (row_ids[:, None] > row_ids[None, :]).astype(jnp.float32)
    same = (row_ids[:, None] == row_ids[None, :]).astype(jnp.float32)
    return lower * below + same * middle[:, None]


def lax_iota(length):
    return jnp.arange(length, dtype=jnp.int32)


def spiked(drawn, own_key, source, target, shards_of, factor):
    def block_of(dim):
        return (jnp.arange(drawn.shape[dim]) // (drawn.shape[dim] // shards_of)).reshape((-1,) + (1,) * (drawn.ndim - 1 - dim))

    near = jax.random.permutation(own_key, shards_of)[block_of(target)]
    far = (block_of(target) + shards_of // 2) % shards_of
    return jnp.where((block_of(source) == near) | (block_of(source) == far), factor * drawn, drawn)


def block_scale(own_key, dims, cuts, smallest, top_value):
    factor_of, own = 1.0, jax.random.fold_in(own_key, 6)
    for dim, blocks in cuts:
        draws = jnp.exp(jax.random.uniform(jax.random.fold_in(own, dim), (blocks,), jnp.float32, smallest / len(cuts), top_value / len(cuts)))
        factor_of = factor_of * jnp.repeat(draws, dims[dim] // blocks).reshape([-1 if axis == dim else 1 for axis in range(len(dims))])
    return factor_of


def gaussian(own_key, dims, width, limit, pieces=(), kind=jnp.bfloat16):
    result = width * jax.random.normal(own_key, dims, jnp.float32)
    if pieces:
        result = result * block_scale(own_key, dims, pieces, -0.22, 0.18)
    return jnp.clip(result, -limit, limit).astype(kind)


def gaussian_with(stream_key, shape, width, bound, pieces, heavy, kind=jnp.bfloat16):
    values = width * jax.random.normal(stream_key, shape, jnp.float32)
    if pieces:
        values = values * block_scale(stream_key, shape, pieces, -0.22, 0.18)
    return jnp.clip(spiked(values, jax.random.fold_in(stream_key, 3), *heavy), -bound, bound).astype(kind)


def setup_inputs(seed: int = 0) -> dict:
    keys = jax.random.split(jax.random.key(seed), 6)
    adjoint_slab = gaussian_with(keys[0], (ROWS, M), 1.0, 16.0, ((0, 8), (1, 64)), (1, 0, 64, 4.0))
    panel_cols = gaussian(keys[1], (M, B), M ** -0.5, 0.0234375, ((0, 64), (1, 8)))
    incoming = gaussian(keys[2], (ROWS, B), 1.0, 6.0, ((0, 512),), jnp.float32)
    inverse_block = draw_inverse_block(jax.random.fold_in(keys[5], 71), 0)
    panel_rows = gaussian(keys[4], (ROWS, B), ROWS ** -0.5, 0.0546875, ((0, 512),))
    return dict(adjoint_slab=adjoint_slab, panel_cols=panel_cols, incoming=incoming, inverse_block=inverse_block, panel_rows=panel_rows)


def reference(adjoint_slab, panel_cols, incoming, inverse_block, panel_rows):
    blocks = adjoint_slab.reshape(N_ROW, ROW_DEV, M)

    def block_product(block):
        return jnp.dot(block, panel_cols, preferred_element_type=jnp.float32)

    product = lax.map(block_product, blocks).reshape(ROWS, B)
    panel_adjoint = incoming - 2.0 * product
    grad_rows = jnp.dot(panel_adjoint, inverse_block, precision=lax.Precision.HIGHEST)
    panel_term = jnp.dot(panel_rows.astype(jnp.float32).T, panel_adjoint, precision=lax.Precision.HIGHEST)
    return grad_rows, panel_term
```

```python
import jax
import jax.numpy as jnp
from jax import lax
from jax.experimental import pallas as pl
from jax.experimental.pallas import tpu as pltpu
from jax.sharding import PartitionSpec as P

MESH = pl.DeviceIdType.MESH
F32, BF16 = jnp.float32, jnp.bfloat16
STEPS = 250.0
HALF = 125.0
COPIES = 96


def encode(value):
    groups = value.reshape(-1, 8, 128)
    size = jnp.abs(groups)
    scale = jnp.maximum(jnp.max(size, axis=0) * 1.004, 1e-30).astype(BF16)
    power = jnp.exp2(size * (STEPS / scale.astype(F32)) - HALF)
    code = jnp.where(groups < 0.0, -power, power).reshape(value.shape)
    scale = scale.astype(F32)
    return jnp.concatenate([code, scale, scale], axis=0).astype(BF16)


def decode(coded):
    coded = coded.astype(F32)
    rows = coded.shape[0] - 16
    groups = coded[:rows].reshape(-1, 8, 128)
    scale = coded[rows : rows + 8] * (1.0 / STEPS)
    steps = jnp.log2(jnp.abs(groups)) + HALF
    return (jnp.where(groups < 0.0, -steps, steps) * scale).reshape(rows, 128)


def kernel(
    a_hbm, b_ref, inc_ref, inv_hbm, p_ref,
    grad_ref, term_ref,
    a, inv, b_sib, b_all, own, xs, xr, ys, yr, ysum, tz, tzr, tx, p_all, p_mat,
    half, half_r, slab, slab_r, zsum, ysl, coded, local_sem, send_sem, recv_sem,
):
    row, col, x = lax.axis_index("row"), lax.axis_index("col"), lax.axis_index("depth")
    zl, c = lax.div(row, 2), lax.rem(row, 2)
    y, zh = lax.div(col, 2), lax.rem(col, 2)
    z = zh * 4 + zl

    def at(x=x, y=y, zh=zh, zl=zl, c=c):
        return (zl * 2 + c, y * 2 + zh, x)

    def x_peer(d):
        return at(x=lax.rem(x + d, 4))

    def y_peer(d):
        return at(y=lax.rem(y + d, 8))

    def z_peer(d):
        other = lax.rem(z + d, 8)
        return at(zh=lax.div(other, 4), zl=lax.rem(other, 4))

    sibling = at(c=1 - c)
    z_far = at(zh=1 - zh)

    load_a = pltpu.make_async_copy(a_hbm, a, local_sem.at[0])
    load_a.start()
    load_inv = pltpu.make_async_copy(inv_hbm, inv, local_sem.at[1])
    load_inv.start()

    barrier = pltpu.get_barrier_semaphore()
    peers = [sibling] + [x_peer(d) for d in range(1, 4)]
    peers += [y_peer(d) for d in range(1, 8)] + [z_peer(d) for d in range(1, 8)]
    for peer in peers:
        pl.semaphore_signal(barrier, inc=1, device_id=peer, device_id_type=MESH)

    wide = jnp.concatenate([p_ref[:, :256].astype(F32), p_ref[:, 256:].astype(F32)], axis=0)
    p_all[x, zh] = wide.astype(BF16)
    pl.semaphore_wait(barrier, len(peers))

    copies = []

    def send(src, dst, target):
        i = len(copies)
        copy = pltpu.make_async_remote_copy(
            src_ref=src, dst_ref=dst, send_sem=send_sem.at[i], recv_sem=recv_sem.at[i],
            device_id=target, device_id_type=MESH,
        )
        copy.start()
        copies.append(copy)
        return copy

    sib = send(b_ref, b_sib, sibling)
    p_far = send(p_all.at[x, zh], p_all.at[x, zh], z_far)
    sib.wait_recv()

    @pl.when(c == 0)
    def _():
        b_all[zl] = jnp.concatenate([b_ref[...], b_sib[...]], axis=1)

    @pl.when(c == 1)
    def _():
        b_all[zl] = jnp.concatenate([b_sib[...], b_ref[...]], axis=1)

    chunk = [zl, zl + 1 - 2 * lax.rem(zl, 2), lax.rem(zl + 2, 4), 3 - zl]
    mine = pl.ds(pl.multiple_of(c * 512, 512), 512)
    line = [None] * 4
    for k in range(1, 4):
        line[k] = send(b_all.at[zl, mine], b_all.at[zl, mine], at(zl=chunk[k]))

    load_a.wait()
    x_copies = [[None] * 4 for _ in range(4)]
    y_copies = [[None] * 8 for _ in range(4)]

    def multiply(k):
        for part in range(2):
            acc = jnp.dot(a[part * 768 : part * 768 + 768, :], b_all[chunk[k]], preferred_element_type=F32)
            for yy in range(4):
                for to in range(4):
                    low = yy * 192 + to * 24
                    own[k, to, (part * 4 + yy) * 48 : (part * 4 + yy) * 48 + 24, :] = acc[low : low + 24]
                    own[k, to, (part * 4 + yy) * 48 + 24 : (part * 4 + yy) * 48 + 48, :] = acc[low + 96 : low + 120]
        for d in (2, 1, 3):
            xs[k, d - 1] = encode(own[k, lax.rem(x + d, 4)])
            x_copies[k][d] = send(xs.at[k, d - 1], xr.at[k, d - 1], x_peer(d))

    def reduce_x(k):
        total = own[k, x]
        for d in (1, 3, 2):
            x_copies[k][d].wait_recv()
            total = total + decode(xr[k, d - 1])
        ysum[k] = total.reshape(8, 48, 128)
        for d in (4, 3, 5, 2, 6, 1, 7):
            ys[k, d - 1] = encode(ysum[k, lax.rem(y + d, 8)])
            y_copies[k][d] = send(ys.at[k, d - 1], yr.at[k, d - 1], y_peer(d))

    def reduce_y(k):
        total = ysum[k, y]
        for d in (1, 7, 2, 6, 3, 5, 4):
            y_copies[k][d].wait_recv()
            total = total + decode(yr[k, d - 1])
        for h in range(2):
            tz[h, chunk[k]] = total[h * 24 : h * 24 + 24] * -2.0

    multiply(0)
    p_far.wait_recv()
    p_copies = [send(p_all.at[x], p_all.at[x], x_peer(d)) for d in range(1, 4)]
    for k in range(1, 4):
        line[k].wait_recv()
        there = b_all.at[chunk[k], mine]
        forward = send(there, there, sibling)
        if k >= 2:
            reduce_x(k - 2)
        forward.wait_recv()
        multiply(k)
    reduce_x(2)
    reduce_y(0)
    reduce_y(1)
    for copy in p_copies:
        copy.wait_recv()
    for i in range(4):
        both = p_all[i].astype(F32)
        rows = [jnp.concatenate([both[h, :24], both[h, 24:]], axis=1) for h in range(2)]
        p_mat[i * 48 : i * 48 + 48, :] = jnp.concatenate(rows, axis=0).astype(BF16)
    reduce_x(3)
    reduce_y(2)
    reduce_y(3)

    far = send(tz.at[1 - zh], tzr, z_far)
    for i in range(4):
        block = inc_ref[:, i * 128 : i * 128 + 128]
        for h in range(2):
            tx[x, i, h * 24 : h * 24 + 24, :] = tz[h, i] + jnp.where(zh == h, block, 0.0)
    t_copies = []
    for d in range(1, 4):
        to = lax.rem(x + d, 4)
        t_copies.append(send(tx.at[x, to], tx.at[x, to], x_peer(d)))
    for copy in t_copies:
        copy.wait_recv()
    blocks = jnp.concatenate([tx[i, x] for i in range(4)], axis=0)
    high = blocks.astype(BF16)
    rest = blocks - high.astype(F32)
    middle = rest.astype(BF16)
    low = (rest - middle.astype(F32)).astype(BF16)
    contrib = jnp.zeros((512, 128), F32)
    for piece in (low, middle, high):
        contrib = contrib + lax.dot_general(p_mat[...], piece, (((0,), (0,)), ((), ())), preferred_element_type=F32)
    half[...] = contrib.reshape(2, 256, 128)
    swap = send(half.at[1 - c], half_r, sibling)

    load_inv.wait()
    far.wait_recv()
    adjoint = jnp.concatenate([tz[zh, i] + tzr[i] for i in range(4)], axis=1) + inc_ref[...]
    swap.wait_recv()
    slab[...] = (half[c] + half_r[...]).reshape(8, 32, 128)
    s_copies = [None] * 8
    for d in (4, 3, 5, 2, 6, 1, 7):
        s_copies[d] = send(slab.at[lax.rem(y + d, 8)], slab_r.at[d - 1], y_peer(d))
    grad_ref[...] = jnp.dot(adjoint, inv[...], precision=lax.Precision.HIGHEST, preferred_element_type=F32)
    total = slab[y]
    for d in (1, 7, 2, 6, 3, 5, 4):
        s_copies[d].wait_recv()
        total = total + slab_r[d - 1]
    zsum[z] = total
    s_copies = [send(zsum.at[z], zsum.at[z], z_peer(d)) for d in (4, 3, 5, 2, 6, 1, 7)]
    for copy in s_copies:
        copy.wait_recv()
    ysl[y] = jnp.sum(zsum[...], axis=0)
    s_copies = [send(ysl.at[y], ysl.at[y], y_peer(d)) for d in (4, 3, 5, 2, 6, 1, 7)]
    for copy in s_copies:
        copy.wait_recv()
    coded[c, x] = encode(ysl[...].reshape(256, 128))
    s_copies = [send(coded.at[c, x], coded.at[c, x], x_peer(d)) for d in (2, 1, 3)]
    last = [send(coded.at[c, x], coded.at[c, x], sibling)]
    for copy, d in zip((s_copies[1], s_copies[2], s_copies[0]), (1, 3, 2)):
        copy.wait_recv()
        source = lax.rem(x - d + 4, 4)
        last.append(send(coded.at[c, source], coded.at[c, source], sibling))
    for copy in last:
        copy.wait_recv()
    term_ref[...] = coded[...]
    for copy in copies:
        copy.wait_send()


def on_device(adjoint_slab, panel_cols, incoming, inverse_block, panel_rows):
    vmem, hbm = pl.BlockSpec(memory_space=pltpu.VMEM), pl.BlockSpec(memory_space=pl.ANY)
    gradient, coded = pl.pallas_call(
        kernel,
        name="panel",
        out_shape=(
            jax.ShapeDtypeStruct((24, 512), F32),
            jax.ShapeDtypeStruct((2, 4, 272, 128), BF16),
        ),
        in_specs=[hbm, vmem, vmem, hbm, vmem],
        out_specs=(vmem, vmem),
        scratch_shapes=[
            pltpu.VMEM((1536, 1024), BF16),
            pltpu.VMEM((512, 512), F32),
            pltpu.VMEM((1024, 64), BF16),
            pltpu.VMEM((4, 1024, 128), BF16),
            pltpu.VMEM((4, 4, 384, 128), F32),
            pltpu.VMEM((4, 3, 400, 128), BF16),
            pltpu.VMEM((4, 3, 400, 128), BF16),
            pltpu.VMEM((4, 7, 64, 128), BF16),
            pltpu.VMEM((4, 7, 64, 128), BF16),
            pltpu.VMEM((4, 8, 48, 128), F32),
            pltpu.VMEM((2, 4, 24, 128), F32),
            pltpu.VMEM((4, 24, 128), F32),
            pltpu.VMEM((4, 4, 48, 128), F32),
            pltpu.VMEM((4, 2, 48, 256), BF16),
            pltpu.VMEM((192, 512), BF16),
            pltpu.VMEM((2, 256, 128), F32),
            pltpu.VMEM((256, 128), F32),
            pltpu.VMEM((8, 32, 128), F32),
            pltpu.VMEM((7, 32, 128), F32),
            pltpu.VMEM((8, 32, 128), F32),
            pltpu.VMEM((8, 32, 128), F32),
            pltpu.VMEM((2, 4, 272, 128), BF16),
            pltpu.SemaphoreType.DMA((2,)),
            pltpu.SemaphoreType.DMA((COPIES,)),
            pltpu.SemaphoreType.DMA((COPIES,)),
        ],
        compiler_params=pltpu.CompilerParams(
            collective_id=0, has_side_effects=True, vmem_limit_bytes=48 << 20
        ),
        cost_estimate=pl.CostEstimate(flops=2 << 30, bytes_accessed=8 << 20, transcendentals=1 << 20),
    )(adjoint_slab, panel_cols, incoming, inverse_block, panel_rows)
    values = coded[:, :, :256].astype(F32).reshape(2, 4, 32, 8, 128)
    scale = coded[:, :, 256:264].astype(F32).reshape(2, 4, 1, 8, 128) * (1.0 / STEPS)
    steps = jnp.log2(jnp.abs(values)) + HALF
    values = jnp.where(values < 0.0, -steps, steps) * scale
    term = values.reshape(2, 4, 256, 128).transpose(0, 2, 1, 3).reshape(512, 512)
    return gradient, term


def solution(mesh):
    return jax.shard_map(
        on_device,
        mesh=mesh,
        in_specs=(
            P("row", ("col", "depth")),
            P(("col", "depth"), "row"),
            P(("row", "col", "depth"), None),
            P(),
            P(("row", "col", "depth"), None),
        ),
        out_specs=(P(("row", "col", "depth"), None), P()),
        check_vma=False,
    )
```

```python
import jax
import jax.numpy as jnp
from jax import lax
from jax.experimental import pallas as pl
from jax.experimental.pallas import tpu as pltpu
from jax.sharding import PartitionSpec as P

MESH = pl.DeviceIdType.MESH
F32, BF16 = jnp.float32, jnp.bfloat16
STEPS = 250.0
HALF = 125.0
COPIES = 128
FAR = (4, 3, 5, 2)
NEAR = (6, 1, 7, 0)


def encode(value):
    groups = value.reshape(-1, 8, 128)
    size = jnp.abs(groups)
    scale = jnp.maximum(jnp.max(size, axis=0) * 1.004, 1e-30).astype(BF16)
    power = jnp.exp2(size * (STEPS / scale.astype(F32)) - HALF)
    code = jnp.where(groups < 0.0, -power, power).reshape(value.shape)
    scale = scale.astype(F32)
    return jnp.concatenate([code, scale, scale], axis=0).astype(BF16)


def decode(coded):
    coded = coded.astype(F32)
    rows = coded.shape[0] - 16
    groups = coded[:rows].reshape(-1, 8, 128)
    scale = coded[rows : rows + 8] * (1.0 / STEPS)
    steps = jnp.log2(jnp.abs(groups)) + HALF
    return (jnp.where(groups < 0.0, -steps, steps) * scale).reshape(rows, 128)


def kernel(
    a_hbm, b_hbm, inc_hbm, inv_hbm, p_hbm,
    grad_ref, term_ref,
    a, inv, inc_ref, p_ref, b_all, own, xs, xr, ys, yr, yown, tz, tzr, tx, p_all, p_mat,
    half, half_r, slab, slab_r, zsum, coded, local_sem, send_sem, recv_sem,
):
    row, col, x = lax.axis_index("row"), lax.axis_index("col"), lax.axis_index("depth")
    zl, c = lax.div(row, 2), lax.rem(row, 2)
    y, zh = lax.div(col, 2), lax.rem(col, 2)
    z = zh * 4 + zl

    def at(x=x, y=y, zh=zh, zl=zl, c=c):
        return (zl * 2 + c, y * 2 + zh, x)

    def x_peer(d):
        return at(x=lax.rem(x + d, 4))

    def y_peer(d):
        return at(y=lax.rem(y + d, 8))

    def z_peer(d):
        other = lax.rem(z + d, 8)
        return at(zh=lax.div(other, 4), zl=lax.rem(other, 4))

    sibling = at(c=1 - c)
    z_far = at(zh=1 - zh)

    mine = pl.ds(pl.multiple_of(c * 64, 64), 64)
    loads = []
    for i, (src, dst) in enumerate((
        (p_hbm, p_ref), (b_hbm, b_all.at[zl, mine]), (a_hbm, a), (inc_hbm, inc_ref), (inv_hbm, inv),
    )):
        loads.append(pltpu.make_async_copy(src, dst, local_sem.at[i]))
        loads[-1].start()
    load_p, load_b, load_a, load_inc, load_inv = loads

    barrier = pltpu.get_barrier_semaphore()
    peers = [sibling] + [x_peer(d) for d in range(1, 4)]
    peers += [y_peer(d) for d in range(1, 8)] + [z_peer(d) for d in range(1, 8)]
    for peer in peers:
        pl.semaphore_signal(barrier, inc=1, device_id=peer, device_id_type=MESH)

    pl.semaphore_wait(barrier, len(peers))

    copies = []

    def plan(src, dst, target, send_index=None, recv_index=None):
        i = len(copies)
        copies.append(None)
        return pltpu.make_async_remote_copy(
            src_ref=src, dst_ref=dst,
            send_sem=send_sem.at[i if send_index is None else send_index],
            recv_sem=recv_sem.at[i if recv_index is None else recv_index],
            device_id=target, device_id_type=MESH,
        )

    def send(src, dst, target):
        copy = plan(src, dst, target)
        copy.start()
        copies[-1] = copy
        return copy

    middle = lax.div(lax.rem(zl, 3) + 1, 2)
    two, three = lax.rem(zl + 2, 4), 3 - zl
    chunk = [
        zl,
        zl + 1 - 2 * lax.rem(zl, 2),
        middle * three + (1 - middle) * two,
        middle * two + (1 - middle) * three,
    ]
    slots = [None, 0, 1 + middle, 2 - middle]
    sib = send(b_hbm, b_all.at[zl, mine], sibling)
    first = len(copies)
    line = [None] + [
        plan(b_hbm, b_all.at[zl, mine], at(zl=chunk[k]), first + k - 1, first + slots[k]) for k in range(1, 4)
    ]
    line[1].start()

    @pl.when(middle == 1)
    def _():
        line[2].start()

    load_p.wait()
    wide = jnp.concatenate([p_ref[:, :256].astype(F32), p_ref[:, 256:].astype(F32)], axis=0)
    p_all[x, zh] = wide.astype(BF16)
    p_far = send(p_all.at[x, zh], p_all.at[x, zh], z_far)
    load_a.wait()
    load_b.wait()
    sib.wait_recv()
    x_copies = {}
    y_copies = {}

    def multiply(k):
        for part in range(2):
            acc = lax.dot_general(
                a[part * 768 : part * 768 + 768, :], b_all[chunk[k]], (((1,), (1,)), ((), ())), preferred_element_type=F32
            )
            for yy in range(4):
                for to in range(4):
                    low = yy * 192 + to * 24
                    own[k, to, part * 4 + yy, :24, :] = acc[low : low + 24]
                    own[k, to, part * 4 + yy, 24:, :] = acc[low + 96 : low + 120]
        for part, order in enumerate((FAR, NEAR)):
            for d in (2, 1, 3):
                xs[k, part, d - 1] = encode(blocks_of(k, lax.rem(x + d, 4), order))
                x_copies[k, part, d] = send(xs.at[k, part, d - 1], xr.at[k, part, d - 1], x_peer(d))

    def blocks_of(k, to, order):
        return jnp.concatenate([own[k, to, lax.rem(y + e, 8)] for e in order], axis=0)

    def reduce_x(k, part):
        order = (FAR, NEAR)[part]
        total = blocks_of(k, x, order)
        for d in (1, 3, 2):
            x_copies[k, part, d].wait_recv()
            total = total + decode(xr[k, part, d - 1])
        for j, d in enumerate(order):
            block = total[j * 48 : j * 48 + 48]
            if d == 0:
                yown[k] = block
            else:
                ys[k, d - 1] = encode(block)
                y_copies[k, d] = send(ys.at[k, d - 1], yr.at[k, d - 1], y_peer(d))

    def reduce_y(k):
        total = yown[k]
        for d in (4, 3, 5, 2, 6, 1, 7):
            y_copies[k, d].wait_recv()
            total = total + decode(yr[k, d - 1])
        for h in range(2):
            tz[h, chunk[k]] = total[h * 24 : h * 24 + 24] * -2.0

    multiply(0)

    @pl.when(middle == 1)
    def _():
        line[2].wait_send()
        line[3].start()

    p_far.wait_recv()
    p_copies = [send(p_all.at[x], p_all.at[x], x_peer(d)) for d in range(1, 4)]
    for k in range(1, 4):
        line[k].wait_recv()
        there = b_all.at[chunk[k], mine]
        forward = send(there, there, sibling)
        if k == 1:

            @pl.when(middle == 0)
            def _():
                line[2].start()

        if k >= 2:
            reduce_x(k - 2, 0)
            reduce_x(k - 2, 1)
        forward.wait_recv()
        multiply(k)
        if k == 1:

            @pl.when(middle == 0)
            def _():
                line[2].wait_send()
                line[3].start()

    reduce_x(2, 0)
    reduce_x(2, 1)
    reduce_y(0)
    reduce_y(1)
    for copy in p_copies:
        copy.wait_recv()
    for i in range(4):
        both = p_all[i].astype(F32)
        rows = [jnp.concatenate([both[h, :24], both[h, 24:]], axis=1) for h in range(2)]
        p_mat[i * 48 : i * 48 + 48, :] = jnp.concatenate(rows, axis=0).astype(BF16)
    reduce_x(3, 0)
    reduce_x(3, 1)
    reduce_y(2)
    reduce_y(3)

    far = send(tz.at[1 - zh], tzr, z_far)
    load_inc.wait()
    for i in range(4):
        block = inc_ref[:, i * 128 : i * 128 + 128]
        for h in range(2):
            tx[x, i, h * 24 : h * 24 + 24, :] = tz[h, i] + jnp.where(zh == h, block, 0.0)
    t_copies = []
    for d in range(1, 4):
        to = lax.rem(x + d, 4)
        t_copies.append(send(tx.at[x, to], tx.at[x, to], x_peer(d)))
    for copy in t_copies:
        copy.wait_recv()
    blocks = jnp.concatenate([tx[i, x] for i in range(4)], axis=0)
    high = blocks.astype(BF16)
    rest = blocks - high.astype(F32)
    middle = rest.astype(BF16)
    low = (rest - middle.astype(F32)).astype(BF16)
    contrib = jnp.zeros((512, 128), F32)
    for piece in (low, middle, high):
        contrib = contrib + lax.dot_general(p_mat[...], piece, (((0,), (0,)), ((), ())), preferred_element_type=F32)
    half[...] = contrib.reshape(2, 256, 128)
    swap = send(half.at[1 - c], half_r, sibling)

    load_inv.wait()
    far.wait_recv()
    adjoint = jnp.concatenate([tz[zh, i] + tzr[i] for i in range(4)], axis=1) + inc_ref[...]
    swap.wait_recv()
    slab[...] = (half[c] + half_r[...]).reshape(8, 32, 128)
    s_copies = [None] * 8
    for d in (4, 3, 5, 2, 6, 1, 7):
        s_copies[d] = send(slab.at[lax.rem(y + d, 8)], slab_r.at[d - 1], y_peer(d))
    grad_ref[...] = jnp.dot(adjoint, inv[...], precision=lax.Precision.HIGHEST, preferred_element_type=F32)
    total = slab[y]
    for d in (1, 7, 2, 6, 3, 5, 4):
        s_copies[d].wait_recv()
        total = total + slab_r[d - 1]
    zsum[z] = total
    s_copies = [send(zsum.at[z], zsum.at[z], z_peer(d)) for d in (4, 3, 5, 2, 6, 1, 7)]
    for copy in s_copies:
        copy.wait_recv()
    coded[c, x, y] = encode(jnp.sum(zsum[...], axis=0))

    def spread(source, d):
        piece = coded.at[c, x, source]
        for e in (2, 1, 3):
            x_copies[d, e] = send(piece, piece, x_peer(e))

    piece = coded.at[c, x, y]
    s_copies = [(d, send(piece, piece, y_peer(d))) for d in (4, 3, 5, 2, 6, 1, 7)]
    spread(y, 0)
    for d, copy in reversed(s_copies):
        copy.wait_recv()
        spread(lax.rem(y - d + 8, 8), d)
    last = [send(coded.at[c, x], coded.at[c, x], sibling)]
    for e in (1, 3, 2):
        for d in (0, 7, 1, 6, 2, 5, 3, 4):
            x_copies[d, e].wait_recv()
        source = lax.rem(x - e + 4, 4)
        last.append(send(coded.at[c, source], coded.at[c, source], sibling))
    for copy in last:
        copy.wait_recv()
    term_ref[...] = coded[...]
    line[1].wait_send()
    line[3].wait_send()
    for copy in copies:
        if copy is not None:
            copy.wait_send()


def finish(grad_in, coded, grad_ref, term_ref, term, sems):
    out = [pltpu.make_async_copy(grad_in, grad_ref, sems.at[0])]
    out[0].start()
    for h in range(2):
        for i in range(4):
            for j in range(8):
                term[h, j * 32 : j * 32 + 32, i * 128 : i * 128 + 128] = decode(coded[h, i, j])
        out.append(pltpu.make_async_copy(term.at[h], term_ref.at[h * 256 : h * 256 + 256], sems.at[1 + h]))
        out[-1].start()
    for copy in out:
        copy.wait()


def on_device(adjoint_slab, panel_cols, incoming, inverse_block, panel_rows):
    vmem, hbm = pl.BlockSpec(memory_space=pltpu.VMEM), pl.BlockSpec(memory_space=pltpu.HBM)
    operands = (adjoint_slab, panel_cols.T, incoming, inverse_block, panel_rows)
    gradient, coded = pl.pallas_call(
        kernel,
        name="panel",
        out_shape=(
            jax.ShapeDtypeStruct((24, 512), F32),
            jax.ShapeDtypeStruct((2, 4, 8, 48, 128), BF16),
        ),
        in_specs=[hbm] * 5,
        out_specs=(vmem, vmem),
        scratch_shapes=[
            pltpu.VMEM((1536, 1024), BF16),
            pltpu.VMEM((512, 512), F32),
            pltpu.VMEM((24, 512), F32),
            pltpu.VMEM((24, 512), BF16),
            pltpu.VMEM((4, 128, 1024), BF16),
            pltpu.VMEM((4, 4, 8, 48, 128), F32),
            pltpu.VMEM((4, 2, 3, 208, 128), BF16),
            pltpu.VMEM((4, 2, 3, 208, 128), BF16),
            pltpu.VMEM((4, 7, 64, 128), BF16),
            pltpu.VMEM((4, 7, 64, 128), BF16),
            pltpu.VMEM((4, 48, 128), F32),
            pltpu.VMEM((2, 4, 24, 128), F32),
            pltpu.VMEM((4, 24, 128), F32),
            pltpu.VMEM((4, 4, 48, 128), F32),
            pltpu.VMEM((4, 2, 48, 256), BF16),
            pltpu.VMEM((192, 512), BF16),
            pltpu.VMEM((2, 256, 128), F32),
            pltpu.VMEM((256, 128), F32),
            pltpu.VMEM((8, 32, 128), F32),
            pltpu.VMEM((7, 32, 128), F32),
            pltpu.VMEM((8, 32, 128), F32),
            pltpu.VMEM((2, 4, 8, 48, 128), BF16),
            pltpu.SemaphoreType.DMA((5,)),
            pltpu.SemaphoreType.DMA((COPIES,)),
            pltpu.SemaphoreType.DMA((COPIES,)),
        ],
        compiler_params=pltpu.CompilerParams(
            collective_id=0, has_side_effects=True, vmem_limit_bytes=40 << 20
        ),
        cost_estimate=pl.CostEstimate(flops=2 << 30, bytes_accessed=8 << 20, transcendentals=1 << 20),
    )(*(pltpu.with_memory_space_constraint(array, pltpu.HBM) for array in operands))
    return pl.pallas_call(
        finish,
        name="finish",
        out_shape=(jax.ShapeDtypeStruct((24, 512), F32), jax.ShapeDtypeStruct((512, 512), F32)),
        in_specs=[vmem, vmem],
        out_specs=(hbm, hbm),
        scratch_shapes=[pltpu.VMEM((2, 256, 512), F32), pltpu.SemaphoreType.DMA((3,))],
    )(gradient, coded)


def solution(mesh):
    return jax.shard_map(
        on_device,
        mesh=mesh,
        in_specs=(
            P("row", ("col", "depth")),
            P(("col", "depth"), "row"),
            P(("row", "col", "depth"), None),
            P(),
            P(("row", "col", "depth"), None),
        ),
        out_specs=(P(("row", "col", "depth"), None), P()),
        check_vma=False,
    )
```

```python
import jax
import jax.numpy as jnp
from jax import lax
from jax.experimental import pallas as pl
from jax.experimental.pallas import tpu as pltpu
from jax.sharding import PartitionSpec as P

MESH = pl.DeviceIdType.MESH
F32, BF16 = jnp.float32, jnp.bfloat16
STEPS = 250.0
HALF = 125.0
COPIES = 128
FAR = (4, 3, 5, 2)
NEAR = (6, 1, 7, 0)


def encode(value):
    groups = value.reshape(-1, 8, 128)
    size = jnp.abs(groups)
    scale = jnp.maximum(jnp.max(size, axis=0) * 1.004, 1e-30).astype(BF16)
    power = jnp.exp2(size * (STEPS / scale.astype(F32)) - HALF)
    code = jnp.where(groups < 0.0, -power, power).reshape(value.shape)
    scale = scale.astype(F32)
    return jnp.concatenate([code, scale, scale], axis=0).astype(BF16)


def decode(coded):
    coded = coded.astype(F32)
    rows = coded.shape[0] - 16
    groups = coded[:rows].reshape(-1, 8, 128)
    scale = coded[rows : rows + 8] * (1.0 / STEPS)
    steps = jnp.log2(jnp.abs(groups)) + HALF
    return (jnp.where(groups < 0.0, -steps, steps) * scale).reshape(rows, 128)


def kernel(
    a_hbm, b_hbm, inc_hbm, inv_hbm, p_hbm,
    grad_ref, term_ref,
    a, inv, inc_ref, p_ref, b_all, own, xs, xr, ys, yr, yown, tz, tzr, tx, p_all, p_mat,
    half, half_r, slab, slab_r, zsum, coded, local_sem, send_sem, recv_sem,
):
    row, col, x = lax.axis_index("row"), lax.axis_index("col"), lax.axis_index("depth")
    zl, c = lax.div(row, 2), lax.rem(row, 2)
    y, zh = lax.div(col, 2), lax.rem(col, 2)
    z = zh * 4 + zl

    def at(x=x, y=y, zh=zh, zl=zl, c=c):
        return (zl * 2 + c, y * 2 + zh, x)

    def x_peer(d):
        return at(x=lax.rem(x + d, 4))

    def y_peer(d):
        return at(y=lax.rem(y + d, 8))

    def z_peer(d):
        other = lax.rem(z + d, 8)
        return at(zh=lax.div(other, 4), zl=lax.rem(other, 4))

    sibling = at(c=1 - c)
    z_far = at(zh=1 - zh)

    mine = pl.ds(pl.multiple_of(c * 64, 64), 64)
    loads = []
    for i, (src, dst) in enumerate((
        (p_hbm, p_ref), (b_hbm, b_all.at[zl, mine]), (a_hbm, a), (inc_hbm, inc_ref), (inv_hbm, inv),
    )):
        loads.append(pltpu.make_async_copy(src, dst, local_sem.at[i]))
        loads[-1].start()
    load_p, load_b, load_a, load_inc, load_inv = loads

    barrier = pltpu.get_barrier_semaphore()
    peers = [sibling] + [x_peer(d) for d in range(1, 4)]
    peers += [y_peer(d) for d in range(1, 8)] + [z_peer(d) for d in range(1, 8)]
    for peer in peers:
        pl.semaphore_signal(barrier, inc=1, device_id=peer, device_id_type=MESH)

    pl.semaphore_wait(barrier, len(peers))

    copies = []

    def plan(src, dst, target, send_index=None, recv_index=None):
        i = len(copies)
        copies.append(None)
        return pltpu.make_async_remote_copy(
            src_ref=src, dst_ref=dst,
            send_sem=send_sem.at[i if send_index is None else send_index],
            recv_sem=recv_sem.at[i if recv_index is None else recv_index],
            device_id=target, device_id_type=MESH,
        )

    def send(src, dst, target):
        copy = plan(src, dst, target)
        copy.start()
        copies[-1] = copy
        return copy

    middle = lax.div(lax.rem(zl, 3) + 1, 2)
    two, three = lax.rem(zl + 2, 4), 3 - zl
    chunk = [
        zl,
        zl + 1 - 2 * lax.rem(zl, 2),
        middle * three + (1 - middle) * two,
        middle * two + (1 - middle) * three,
    ]
    slots = [None, 0, 1 + middle, 2 - middle]
    sib = send(b_hbm, b_all.at[zl, mine], sibling)
    first = len(copies)
    line = [None] + [
        plan(b_hbm, b_all.at[zl, mine], at(zl=chunk[k]), first + k - 1, first + slots[k]) for k in range(1, 4)
    ]
    line[1].start()

    @pl.when(middle == 1)
    def _():
        line[2].start()

    load_p.wait()
    wide = jnp.concatenate([p_ref[:, :256].astype(F32), p_ref[:, 256:].astype(F32)], axis=0)
    p_all[x, zh] = wide.astype(BF16)
    p_far = send(p_all.at[x, zh], p_all.at[x, zh], z_far)
    p_copies = [send(p_all.at[x, zh], p_all.at[x, zh], x_peer(d)) for d in range(1, 4)]
    load_a.wait()
    load_b.wait()
    sib.wait_recv()
    x_copies = {}
    y_copies = {}

    def multiply(k):
        for part in range(2):
            acc = lax.dot_general(
                a[part * 768 : part * 768 + 768, :], b_all[chunk[k]], (((1,), (1,)), ((), ())), preferred_element_type=F32
            )
            for yy in range(4):
                for to in range(4):
                    low = yy * 192 + to * 24
                    own[k, to, part * 4 + yy, :24, :] = acc[low : low + 24]
                    own[k, to, part * 4 + yy, 24:, :] = acc[low + 96 : low + 120]
        for part, order in enumerate((FAR, NEAR)):
            for d in (2, 1, 3):
                xs[k, part, d - 1] = encode(blocks_of(k, lax.rem(x + d, 4), order))
                x_copies[k, part, d] = send(xs.at[k, part, d - 1], xr.at[k, part, d - 1], x_peer(d))

    def blocks_of(k, to, order):
        return jnp.concatenate([own[k, to, lax.rem(y + e, 8)] for e in order], axis=0)

    def reduce_x(k, part):
        order = (FAR, NEAR)[part]
        total = blocks_of(k, x, order)
        for d in (1, 3, 2):
            x_copies[k, part, d].wait_recv()
            total = total + decode(xr[k, part, d - 1])
        for j, d in enumerate(order):
            block = total[j * 48 : j * 48 + 48]
            if d == 0:
                yown[k] = block
            else:
                ys[k, d - 1] = encode(block)
                y_copies[k, d] = send(ys.at[k, d - 1], yr.at[k, d - 1], y_peer(d))

    def reduce_y(k):
        total = yown[k]
        for d in (4, 3, 5, 2, 6, 1, 7):
            y_copies[k, d].wait_recv()
            total = total + decode(yr[k, d - 1])
        for h in range(2):
            tz[h, chunk[k]] = total[h * 24 : h * 24 + 24] * -2.0

    multiply(0)

    @pl.when(middle == 1)
    def _():
        line[2].wait_send()
        line[3].start()

    def arrive(k):
        line[k].wait_recv()
        there = b_all.at[chunk[k], mine]
        return send(there, there, sibling)

    forward = arrive(1)

    @pl.when(middle == 0)
    def _():
        line[2].start()

    forward.wait_recv()
    multiply(1)

    @pl.when(middle == 0)
    def _():
        line[2].wait_send()
        line[3].start()

    forward = arrive(2)
    reduce_x(0, 0)
    reduce_x(0, 1)
    forward.wait_recv()
    multiply(2)
    forward = arrive(3)
    p_far.wait_recv()
    p_copies += [send(p_all.at[x, 1 - zh], p_all.at[x, 1 - zh], x_peer(d)) for d in range(1, 4)]
    forward.wait_recv()
    multiply(3)
    reduce_x(1, 0)
    reduce_x(1, 1)
    reduce_x(2, 0)
    reduce_x(2, 1)
    reduce_y(0)
    reduce_y(1)
    for copy in p_copies:
        copy.wait_recv()
    for i in range(4):
        both = p_all[i].astype(F32)
        rows = [jnp.concatenate([both[h, :24], both[h, 24:]], axis=1) for h in range(2)]
        p_mat[i * 48 : i * 48 + 48, :] = jnp.concatenate(rows, axis=0).astype(BF16)
    reduce_x(3, 0)
    reduce_x(3, 1)
    reduce_y(2)
    reduce_y(3)

    far = send(tz.at[1 - zh], tzr, z_far)
    load_inc.wait()
    for i in range(4):
        block = inc_ref[:, i * 128 : i * 128 + 128]
        for h in range(2):
            tx[x, i, h * 24 : h * 24 + 24, :] = tz[h, i] + jnp.where(zh == h, block, 0.0)
    t_copies = []
    for d in range(1, 4):
        to = lax.rem(x + d, 4)
        t_copies.append(send(tx.at[x, to], tx.at[x, to], x_peer(d)))
    for copy in t_copies:
        copy.wait_recv()
    blocks = jnp.concatenate([tx[i, x] for i in range(4)], axis=0)
    high = blocks.astype(BF16)
    rest = blocks - high.astype(F32)
    middle = rest.astype(BF16)
    low = (rest - middle.astype(F32)).astype(BF16)
    contrib = jnp.zeros((512, 128), F32)
    for piece in (low, middle, high):
        contrib = contrib + lax.dot_general(p_mat[...], piece, (((0,), (0,)), ((), ())), preferred_element_type=F32)
    half[...] = contrib.reshape(2, 256, 128)
    swap = send(half.at[1 - c], half_r, sibling)

    load_inv.wait()
    far.wait_recv()
    adjoint = jnp.concatenate([tz[zh, i] + tzr[i] for i in range(4)], axis=1) + inc_ref[...]
    swap.wait_recv()
    slab[...] = (half[c] + half_r[...]).reshape(8, 32, 128)
    s_copies = [None] * 8
    for d in (4, 3, 5, 2, 6, 1, 7):
        s_copies[d] = send(slab.at[lax.rem(y + d, 8)], slab_r.at[d - 1], y_peer(d))
    grad_ref[...] = jnp.dot(adjoint, inv[...], precision=lax.Precision.HIGHEST, preferred_element_type=F32)
    total = slab[y]
    for d in (1, 7, 2, 6, 3, 5, 4):
        s_copies[d].wait_recv()
        total = total + slab_r[d - 1]
    zsum[z] = total
    s_copies = [send(zsum.at[z], zsum.at[z], z_peer(d)) for d in (4, 3, 5, 2, 6, 1, 7)]
    for copy in s_copies:
        copy.wait_recv()
    coded[c, x, y] = encode(jnp.sum(zsum[...], axis=0))

    def spread(source, d):
        piece = coded.at[c, x, source]
        for e in (2, 1, 3):
            x_copies[d, e] = send(piece, piece, x_peer(e))

    piece = coded.at[c, x, y]
    s_copies = [(d, send(piece, piece, y_peer(d))) for d in (4, 3, 5, 2, 6, 1, 7)]
    spread(y, 0)
    for d, copy in reversed(s_copies):
        copy.wait_recv()
        spread(lax.rem(y - d + 8, 8), d)
    last = [send(coded.at[c, x], coded.at[c, x], sibling)]
    for e in (1, 3, 2):
        for d in (0, 7, 1, 6, 2, 5, 3, 4):
            x_copies[d, e].wait_recv()
        source = lax.rem(x - e + 4, 4)
        last.append(send(coded.at[c, source], coded.at[c, source], sibling))
    for copy in last:
        copy.wait_recv()
    for h in range(2):
        for i in range(4):
            for j in range(8):
                low = h * 256 + j * 32
                term_ref[low : low + 32, i * 128 : i * 128 + 128] = decode(coded[h, i, j])
    line[1].wait_send()
    line[3].wait_send()
    for copy in copies:
        if copy is not None:
            copy.wait_send()


def on_device(adjoint_slab, panel_cols, incoming, inverse_block, panel_rows):
    vmem, hbm = pl.BlockSpec(memory_space=pltpu.VMEM), pl.BlockSpec(memory_space=pltpu.HBM)
    operands = (adjoint_slab, panel_cols.T, incoming, inverse_block, panel_rows)
    return pl.pallas_call(
        kernel,
        name="panel",
        out_shape=(
            pltpu.VMEM((24, 512), F32),
            pltpu.VMEM((512, 512), F32),
        ),
        in_specs=[hbm] * 5,
        out_specs=(vmem, vmem),
        scratch_shapes=[
            pltpu.VMEM((1536, 1024), BF16),
            pltpu.VMEM((512, 512), F32),
            pltpu.VMEM((24, 512), F32),
            pltpu.VMEM((24, 512), BF16),
            pltpu.VMEM((4, 128, 1024), BF16),
            pltpu.VMEM((4, 4, 8, 48, 128), F32),
            pltpu.VMEM((4, 2, 3, 208, 128), BF16),
            pltpu.VMEM((4, 2, 3, 208, 128), BF16),
            pltpu.VMEM((4, 7, 64, 128), BF16),
            pltpu.VMEM((4, 7, 64, 128), BF16),
            pltpu.VMEM((4, 48, 128), F32),
            pltpu.VMEM((2, 4, 24, 128), F32),
            pltpu.VMEM((4, 24, 128), F32),
            pltpu.VMEM((4, 4, 48, 128), F32),
            pltpu.VMEM((4, 2, 48, 256), BF16),
            pltpu.VMEM((192, 512), BF16),
            pltpu.VMEM((2, 256, 128), F32),
            pltpu.VMEM((256, 128), F32),
            pltpu.VMEM((8, 32, 128), F32),
            pltpu.VMEM((7, 32, 128), F32),
            pltpu.VMEM((8, 32, 128), F32),
            pltpu.VMEM((2, 4, 8, 48, 128), BF16),
            pltpu.SemaphoreType.DMA((5,)),
            pltpu.SemaphoreType.DMA((COPIES,)),
            pltpu.SemaphoreType.DMA((COPIES,)),
        ],
        compiler_params=pltpu.CompilerParams(
            collective_id=0, has_side_effects=True, vmem_limit_bytes=40 << 20
        ),
        cost_estimate=pl.CostEstimate(flops=2 << 30, bytes_accessed=8 << 20, transcendentals=1 << 20),
    )(*(pltpu.with_memory_space_constraint(array, pltpu.HBM) for array in operands))

def solution(mesh):
    return jax.shard_map(
        on_device,
        mesh=mesh,
        in_specs=(
            P("row", ("col", "depth")),
            P(("col", "depth"), "row"),
            P(("row", "col", "depth"), None),
            P(),
            P(("row", "col", "depth"), None),
        ),
        out_specs=(P(("row", "col", "depth"), None), P()),
        check_vma=False,
    )
```

```python
import jax
import jax.numpy as jnp
from jax import lax
from jax.experimental import pallas as pl
from jax.experimental.pallas import tpu as pltpu
from jax.sharding import PartitionSpec as P

MESH = pl.DeviceIdType.MESH
F32, BF16 = jnp.float32, jnp.bfloat16
STEPS = 250.0
HALF = 125.0
COPIES = 128
FAR = (4, 3, 5, 2)
NEAR = (6, 1, 7, 0)


def encode(value):
    groups = value.reshape(-1, 8, 128)
    size = jnp.abs(groups)
    scale = jnp.maximum(jnp.max(size, axis=0) * 1.004, 1e-30).astype(BF16)
    power = jnp.exp2(size * (STEPS / scale.astype(F32)) - HALF)
    code = jnp.where(groups < 0.0, -power, power).reshape(value.shape)
    scale = scale.astype(F32)
    return jnp.concatenate([code, scale, scale], axis=0).astype(BF16)


def decode(coded):
    coded = coded.astype(F32)
    rows = coded.shape[0] - 16
    groups = coded[:rows].reshape(-1, 8, 128)
    scale = coded[rows : rows + 8] * (1.0 / STEPS)
    steps = jnp.log2(jnp.abs(groups)) + HALF
    return (jnp.where(groups < 0.0, -steps, steps) * scale).reshape(rows, 128)


def kernel(
    a_hbm, b_hbm, inc_hbm, inv_hbm, p_hbm,
    grad_ref, term_ref,
    a, inv, inc_ref, p_ref, b_all, own, xs, xr, ys, yr, yown, tz, tzr, tx, p_all, p_mat,
    half, half_r, slab, slab_r, zsum, coded, local_sem, send_sem, recv_sem,
):
    row, col, x = lax.axis_index("row"), lax.axis_index("col"), lax.axis_index("depth")
    zl, c = lax.div(row, 2), lax.rem(row, 2)
    y, zh = lax.div(col, 2), lax.rem(col, 2)
    z = zh * 4 + zl

    def at(x=x, y=y, zh=zh, zl=zl, c=c):
        return (zl * 2 + c, y * 2 + zh, x)

    def x_peer(d):
        return at(x=lax.rem(x + d, 4))

    def y_peer(d):
        return at(y=lax.rem(y + d, 8))

    def z_peer(d):
        other = lax.rem(z + d, 8)
        return at(zh=lax.div(other, 4), zl=lax.rem(other, 4))

    sibling = at(c=1 - c)
    z_far = at(zh=1 - zh)

    mine = pl.ds(pl.multiple_of(c * 64, 64), 64)
    loads = []
    for i, (src, dst) in enumerate((
        (p_hbm, p_ref), (b_hbm, b_all.at[zl, mine]), (a_hbm, a), (inc_hbm, inc_ref), (inv_hbm, inv),
    )):
        loads.append(pltpu.make_async_copy(src, dst, local_sem.at[i]))
        loads[-1].start()
    load_p, load_b, load_a, load_inc, load_inv = loads

    barrier = pltpu.get_barrier_semaphore()
    peers = [sibling] + [x_peer(d) for d in range(1, 4)]
    peers += [y_peer(d) for d in range(1, 8)] + [z_peer(d) for d in range(1, 8)]
    for peer in peers:
        pl.semaphore_signal(barrier, inc=1, device_id=peer, device_id_type=MESH)

    pl.semaphore_wait(barrier, len(peers))

    copies = []

    def plan(src, dst, target, send_index=None, recv_index=None):
        i = len(copies)
        copies.append(None)
        return pltpu.make_async_remote_copy(
            src_ref=src, dst_ref=dst,
            send_sem=send_sem.at[i if send_index is None else send_index],
            recv_sem=recv_sem.at[i if recv_index is None else recv_index],
            device_id=target, device_id_type=MESH,
        )

    def send(src, dst, target):
        copy = plan(src, dst, target)
        copy.start()
        copies[-1] = copy
        return copy

    middle = lax.div(lax.rem(zl, 3) + 1, 2)
    two, three = lax.rem(zl + 2, 4), 3 - zl
    chunk = [
        zl,
        zl + 1 - 2 * lax.rem(zl, 2),
        middle * three + (1 - middle) * two,
        middle * two + (1 - middle) * three,
    ]
    slots = [None, 0, 1 + middle, 2 - middle]
    sib = send(b_hbm, b_all.at[zl, mine], sibling)
    first = len(copies)
    line = [None] + [
        plan(b_hbm, b_all.at[zl, mine], at(zl=chunk[k]), first + k - 1, first + slots[k]) for k in range(1, 4)
    ]
    line[1].start()

    @pl.when(middle == 1)
    def _():
        line[2].start()

    load_p.wait()
    wide = jnp.concatenate([p_ref[:, :256].astype(F32), p_ref[:, 256:].astype(F32)], axis=0)
    p_all[x, zh] = wide.astype(BF16)
    p_far = send(p_all.at[x, zh], p_all.at[x, zh], z_far)
    p_copies = [send(p_all.at[x, zh], p_all.at[x, zh], x_peer(d)) for d in range(1, 4)]
    load_a.wait()
    load_b.wait()
    sib.wait_recv()
    x_copies = {}
    y_copies = {}

    def multiply(k):
        for part in range(2):
            acc = lax.dot_general(
                a[part * 768 : part * 768 + 768, :], b_all[chunk[k]], (((1,), (1,)), ((), ())), preferred_element_type=F32
            )
            for yy in range(4):
                for to in range(4):
                    low = yy * 192 + to * 24
                    own[k, to, part * 4 + yy, :24, :] = acc[low : low + 24]
                    own[k, to, part * 4 + yy, 24:, :] = acc[low + 96 : low + 120]
        for part, order in enumerate((FAR, NEAR)):
            for d in (2, 1, 3):
                xs[k, part, d - 1] = encode(blocks_of(k, lax.rem(x + d, 4), order))
                x_copies[k, part, d] = send(xs.at[k, part, d - 1], xr.at[k, part, d - 1], x_peer(d))

    def blocks_of(k, to, order):
        return jnp.concatenate([own[k, to, lax.rem(y + e, 8)] for e in order], axis=0)

    def reduce_x(k, part):
        order = (FAR, NEAR)[part]
        total = blocks_of(k, x, order)
        for d in (1, 3, 2):
            x_copies[k, part, d].wait_recv()
            total = total + decode(xr[k, part, d - 1])
        for j, d in enumerate(order):
            block = total[j * 48 : j * 48 + 48]
            if d == 0:
                yown[k] = block
            else:
                ys[k, d - 1] = encode(block)
                y_copies[k, d] = send(ys.at[k, d - 1], yr.at[k, d - 1], y_peer(d))

    def reduce_y(k):
        total = yown[k]
        for d in (4, 3, 5, 2, 6, 1, 7):
            y_copies[k, d].wait_recv()
            total = total + decode(yr[k, d - 1])
        for h in range(2):
            tz[h, chunk[k]] = total[h * 24 : h * 24 + 24] * -2.0

    multiply(0)

    @pl.when(middle == 1)
    def _():
        line[2].wait_send()
        line[3].start()

    def arrive(k):
        line[k].wait_recv()
        there = b_all.at[chunk[k], mine]
        return send(there, there, sibling)

    forward = arrive(1)
    p_far.wait_recv()
    p_copies += [send(p_all.at[x, 1 - zh], p_all.at[x, 1 - zh], x_peer(d)) for d in range(1, 4)]

    @pl.when(middle == 0)
    def _():
        line[2].start()

    forward.wait_recv()
    multiply(1)

    @pl.when(middle == 0)
    def _():
        line[2].wait_send()
        line[3].start()

    forward = arrive(2)
    reduce_x(0, 0)
    reduce_x(0, 1)
    forward.wait_recv()
    multiply(2)
    forward = arrive(3)
    forward.wait_recv()
    multiply(3)
    reduce_x(1, 0)
    reduce_x(1, 1)
    reduce_x(2, 0)
    reduce_x(2, 1)
    for copy in p_copies:
        copy.wait_recv()
    for i in range(4):
        both = p_all[i].astype(F32)
        rows = [jnp.concatenate([both[h, :24], both[h, 24:]], axis=1) for h in range(2)]
        p_mat[i * 48 : i * 48 + 48, :] = jnp.concatenate(rows, axis=0).astype(BF16)
    reduce_x(3, 0)
    reduce_x(3, 1)
    reduce_y(0)
    reduce_y(1)
    reduce_y(2)
    reduce_y(3)

    far = send(tz.at[1 - zh], tzr, z_far)
    load_inc.wait()
    for i in range(4):
        block = inc_ref[:, i * 128 : i * 128 + 128]
        for h in range(2):
            tx[x, i, h * 24 : h * 24 + 24, :] = tz[h, i] + jnp.where(zh == h, block, 0.0)
    t_copies = []
    for d in range(1, 4):
        to = lax.rem(x + d, 4)
        t_copies.append(send(tx.at[x, to], tx.at[x, to], x_peer(d)))
    for copy in t_copies:
        copy.wait_recv()
    blocks = jnp.concatenate([tx[i, x] for i in range(4)], axis=0)
    high = blocks.astype(BF16)
    rest = blocks - high.astype(F32)
    middle = rest.astype(BF16)
    low = (rest - middle.astype(F32)).astype(BF16)
    contrib = jnp.zeros((512, 128), F32)
    for piece in (low, middle, high):
        contrib = contrib + lax.dot_general(p_mat[...], piece, (((0,), (0,)), ((), ())), preferred_element_type=F32)
    half[...] = contrib.reshape(2, 256, 128)
    swap = send(half.at[1 - c], half_r, sibling)

    load_inv.wait()
    far.wait_recv()
    adjoint = jnp.concatenate([tz[zh, i] + tzr[i] for i in range(4)], axis=1) + inc_ref[...]
    swap.wait_recv()
    slab[...] = (half[c] + half_r[...]).reshape(8, 32, 128)
    s_copies = [None] * 8
    for d in (4, 3, 5, 2, 6, 1, 7):
        s_copies[d] = send(slab.at[lax.rem(y + d, 8)], slab_r.at[d - 1], y_peer(d))
    grad_ref[...] = jnp.dot(adjoint, inv[...], precision=lax.Precision.HIGHEST, preferred_element_type=F32)
    total = slab[y]
    for d in (1, 7, 2, 6, 3, 5, 4):
        s_copies[d].wait_recv()
        total = total + slab_r[d - 1]
    zsum[z] = total
    s_copies = [send(zsum.at[z], zsum.at[z], z_peer(d)) for d in (4, 3, 5, 2, 6, 1, 7)]
    for copy in s_copies:
        copy.wait_recv()
    coded[c, x, y] = encode(jnp.sum(zsum[...], axis=0))

    def spread(source, d):
        piece = coded.at[c, x, source]
        for e in (2, 1, 3):
            x_copies[d, e] = send(piece, piece, x_peer(e))

    piece = coded.at[c, x, y]
    s_copies = [(d, send(piece, piece, y_peer(d))) for d in (4, 3, 5, 2, 6, 1, 7)]
    spread(y, 0)
    for d, copy in reversed(s_copies):
        copy.wait_recv()
        spread(lax.rem(y - d + 8, 8), d)
    last = [send(coded.at[c, x], coded.at[c, x], sibling)]
    for e in (1, 3, 2):
        for d in (0, 7, 1, 6, 2, 5, 3, 4):
            x_copies[d, e].wait_recv()
        source = lax.rem(x - e + 4, 4)
        last.append(send(coded.at[c, source], coded.at[c, source], sibling))
    for copy in last:
        copy.wait_recv()
    for h in range(2):
        for i in range(4):
            for j in range(8):
                low = h * 256 + j * 32
                term_ref[low : low + 32, i * 128 : i * 128 + 128] = decode(coded[h, i, j])
    line[1].wait_send()
    line[3].wait_send()
    for copy in copies:
        if copy is not None:
            copy.wait_send()


def on_device(adjoint_slab, panel_cols, incoming, inverse_block, panel_rows):
    vmem, hbm = pl.BlockSpec(memory_space=pltpu.VMEM), pl.BlockSpec(memory_space=pltpu.HBM)
    operands = (adjoint_slab, panel_cols.T, incoming, inverse_block, panel_rows)
    return pl.pallas_call(
        kernel,
        name="panel",
        out_shape=(
            pltpu.VMEM((24, 512), F32),
            pltpu.VMEM((512, 512), F32),
        ),
        in_specs=[hbm] * 5,
        out_specs=(vmem, vmem),
        scratch_shapes=[
            pltpu.VMEM((1536, 1024), BF16),
            pltpu.VMEM((512, 512), F32),
            pltpu.VMEM((24, 512), F32),
            pltpu.VMEM((24, 512), BF16),
            pltpu.VMEM((4, 128, 1024), BF16),
            pltpu.VMEM((4, 4, 8, 48, 128), F32),
            pltpu.VMEM((4, 2, 3, 208, 128), BF16),
            pltpu.VMEM((4, 2, 3, 208, 128), BF16),
            pltpu.VMEM((4, 7, 64, 128), BF16),
            pltpu.VMEM((4, 7, 64, 128), BF16),
            pltpu.VMEM((4, 48, 128), F32),
            pltpu.VMEM((2, 4, 24, 128), F32),
            pltpu.VMEM((4, 24, 128), F32),
            pltpu.VMEM((4, 4, 48, 128), F32),
            pltpu.VMEM((4, 2, 48, 256), BF16),
            pltpu.VMEM((192, 512), BF16),
            pltpu.VMEM((2, 256, 128), F32),
            pltpu.VMEM((256, 128), F32),
            pltpu.VMEM((8, 32, 128), F32),
            pltpu.VMEM((7, 32, 128), F32),
            pltpu.VMEM((8, 32, 128), F32),
            pltpu.VMEM((2, 4, 8, 48, 128), BF16),
            pltpu.SemaphoreType.DMA((5,)),
            pltpu.SemaphoreType.DMA((COPIES,)),
            pltpu.SemaphoreType.DMA((COPIES,)),
        ],
        compiler_params=pltpu.CompilerParams(
            collective_id=0, has_side_effects=True, vmem_limit_bytes=40 << 20
        ),
        cost_estimate=pl.CostEstimate(flops=2 << 30, bytes_accessed=8 << 20, transcendentals=1 << 20),
    )(*(pltpu.with_memory_space_constraint(array, pltpu.HBM) for array in operands))

def solution(mesh):
    return jax.shard_map(
        on_device,
        mesh=mesh,
        in_specs=(
            P("row", ("col", "depth")),
            P(("col", "depth"), "row"),
            P(("row", "col", "depth"), None),
            P(),
            P(("row", "col", "depth"), None),
        ),
        out_specs=(P(("row", "col", "depth"), None), P()),
        check_vma=False,
    )
```

```python
import jax
import jax.numpy as jnp
from jax import lax
from jax.experimental import pallas as pl
from jax.experimental.pallas import tpu as pltpu
from jax.sharding import PartitionSpec as P

MESH = pl.DeviceIdType.MESH
F32, BF16 = jnp.float32, jnp.bfloat16
STEPS = 250.0
HALF = 125.0
COPIES = 128
FAR = (4, 3, 5, 2)
NEAR = (6, 1, 7, 0)


def encode(value):
    groups = value.reshape(-1, 8, 128)
    size = jnp.abs(groups)
    scale = jnp.maximum(jnp.max(size, axis=0) * 1.004, 1e-30).astype(BF16)
    power = jnp.exp2(size * (STEPS / scale.astype(F32)) - HALF)
    code = jnp.where(groups < 0.0, -power, power).reshape(value.shape)
    scale = scale.astype(F32)
    return jnp.concatenate([code, scale, scale], axis=0).astype(BF16)


def decode(coded):
    coded = coded.astype(F32)
    rows = coded.shape[0] - 16
    groups = coded[:rows].reshape(-1, 8, 128)
    scale = coded[rows : rows + 8] * (1.0 / STEPS)
    steps = jnp.log2(jnp.abs(groups)) + HALF
    return (jnp.where(groups < 0.0, -steps, steps) * scale).reshape(rows, 128)


def kernel(
    a_hbm, b_hbm, inc_hbm, inv_hbm, p_hbm,
    grad_ref, term_ref,
    a, inv, inc_ref, p_ref, b_all, own, xs, xr, ys, yr, yown, tz, tzr, tx, p_all, p_mat,
    half, half_r, slab, slab_r, zsum, coded, local_sem, send_sem, recv_sem,
):
    row, col, x = lax.axis_index("row"), lax.axis_index("col"), lax.axis_index("depth")
    zl, c = lax.div(row, 2), lax.rem(row, 2)
    y, zh = lax.div(col, 2), lax.rem(col, 2)
    z = zh * 4 + zl

    def at(x=x, y=y, zh=zh, zl=zl, c=c):
        return (zl * 2 + c, y * 2 + zh, x)

    def x_peer(d):
        return at(x=lax.rem(x + d, 4))

    def y_peer(d):
        return at(y=lax.rem(y + d, 8))

    def z_peer(d):
        other = lax.rem(z + d, 8)
        return at(zh=lax.div(other, 4), zl=lax.rem(other, 4))

    sibling = at(c=1 - c)
    z_far = at(zh=1 - zh)

    mine = pl.ds(pl.multiple_of(c * 64, 64), 64)
    loads = []
    for i, (src, dst) in enumerate((
        (p_hbm, p_ref), (b_hbm, b_all.at[zl, mine]), (a_hbm, a), (inc_hbm, inc_ref), (inv_hbm, inv),
    )):
        loads.append(pltpu.make_async_copy(src, dst, local_sem.at[i]))
        loads[-1].start()
    load_p, load_b, load_a, load_inc, load_inv = loads

    barrier = pltpu.get_barrier_semaphore()
    peers = [sibling] + [x_peer(d) for d in range(1, 4)]
    peers += [y_peer(d) for d in range(1, 8)] + [z_peer(d) for d in range(1, 8)]
    for peer in peers:
        pl.semaphore_signal(barrier, inc=1, device_id=peer, device_id_type=MESH)

    pl.semaphore_wait(barrier, len(peers))

    copies = []

    def plan(src, dst, target, send_index=None, recv_index=None):
        i = len(copies)
        copies.append(None)
        return pltpu.make_async_remote_copy(
            src_ref=src, dst_ref=dst,
            send_sem=send_sem.at[i if send_index is None else send_index],
            recv_sem=recv_sem.at[i if recv_index is None else recv_index],
            device_id=target, device_id_type=MESH,
        )

    def send(src, dst, target):
        copy = plan(src, dst, target)
        copy.start()
        copies[-1] = copy
        return copy

    middle = lax.div(lax.rem(zl, 3) + 1, 2)
    two, three = lax.rem(zl + 2, 4), 3 - zl
    chunk = [
        zl,
        zl + 1 - 2 * lax.rem(zl, 2),
        middle * three + (1 - middle) * two,
        middle * two + (1 - middle) * three,
    ]
    slots = [None, 0, 1 + middle, 2 - middle]
    sib = send(b_hbm, b_all.at[zl, mine], sibling)
    first = len(copies)
    line = [None] + [
        plan(b_hbm, b_all.at[zl, mine], at(zl=chunk[k]), first + k - 1, first + slots[k]) for k in range(1, 4)
    ]
    line[1].start()

    @pl.when(middle == 1)
    def _():
        line[2].start()

    load_p.wait()
    wide = jnp.concatenate([p_ref[:, :256].astype(F32), p_ref[:, 256:].astype(F32)], axis=0)
    p_all[x, zh] = wide.astype(BF16)
    p_far = send(p_all.at[x, zh], p_all.at[x, zh], z_far)
    p_copies = [send(p_all.at[x, zh], p_all.at[x, zh], x_peer(d)) for d in range(1, 4)]
    load_a.wait()
    load_b.wait()
    sib.wait_recv()
    x_copies = {}
    y_copies = {}

    def multiply(k):
        for part in range(2):
            acc = lax.dot_general(
                a[part * 768 : part * 768 + 768, :], b_all[chunk[k]], (((1,), (1,)), ((), ())), preferred_element_type=F32
            )
            for yy in range(4):
                for to in range(4):
                    low = yy * 192 + to * 24
                    own[k, to, part * 4 + yy, :24, :] = acc[low : low + 24]
                    own[k, to, part * 4 + yy, 24:, :] = acc[low + 96 : low + 120]
        for part, order in enumerate((FAR, NEAR)):
            for d in (2, 1, 3):
                xs[k, part, d - 1] = encode(blocks_of(k, lax.rem(x + d, 4), order))
                x_copies[k, part, d] = send(xs.at[k, part, d - 1], xr.at[k, part, d - 1], x_peer(d))

    def blocks_of(k, to, order):
        return jnp.concatenate([own[k, to, lax.rem(y + e, 8)] for e in order], axis=0)

    def reduce_x(k, part):
        order = (FAR, NEAR)[part]
        total = blocks_of(k, x, order)
        for d in (1, 3, 2):
            x_copies[k, part, d].wait_recv()
            total = total + decode(xr[k, part, d - 1])
        for j, d in enumerate(order):
            block = total[j * 48 : j * 48 + 48]
            if d == 0:
                yown[k] = block
            else:
                ys[k, d - 1] = encode(block)
                y_copies[k, d] = send(ys.at[k, d - 1], yr.at[k, d - 1], y_peer(d))

    def reduce_y(k):
        total = yown[k]
        for d in (4, 3, 5, 2, 6, 1, 7):
            y_copies[k, d].wait_recv()
            total = total + decode(yr[k, d - 1])
        for h in range(2):
            tz[h, chunk[k]] = total[h * 24 : h * 24 + 24] * -2.0

    multiply(0)

    @pl.when(middle == 1)
    def _():
        line[2].wait_send()
        line[3].start()

    def arrive(k):
        line[k].wait_recv()
        there = b_all.at[chunk[k], mine]
        return send(there, there, sibling)

    forward = arrive(1)
    p_far.wait_recv()
    p_copies += [send(p_all.at[x, 1 - zh], p_all.at[x, 1 - zh], x_peer(d)) for d in range(1, 4)]

    @pl.when(middle == 0)
    def _():
        line[2].start()

    forward.wait_recv()
    multiply(1)

    @pl.when(middle == 0)
    def _():
        line[2].wait_send()
        line[3].start()

    forward = arrive(2)
    reduce_x(0, 0)
    reduce_x(0, 1)
    forward.wait_recv()
    multiply(2)
    forward = arrive(3)
    forward.wait_recv()
    multiply(3)
    reduce_x(1, 0)
    reduce_x(1, 1)
    reduce_x(2, 0)
    reduce_x(2, 1)
    for copy in p_copies:
        copy.wait_recv()
    for i in range(4):
        both = p_all[i].astype(F32)
        rows = [jnp.concatenate([both[h, :24], both[h, 24:]], axis=1) for h in range(2)]
        p_mat[i * 48 : i * 48 + 48, :] = jnp.concatenate(rows, axis=0).astype(BF16)
    reduce_x(3, 0)
    reduce_x(3, 1)
    reduce_y(0)
    reduce_y(1)
    reduce_y(2)
    reduce_y(3)

    load_inc.wait()
    for i in range(4):
        block = inc_ref[:, i * 128 : i * 128 + 128]
        for h in range(2):
            tx[x, i, h * 24 : h * 24 + 24, :] = tz[h, i] + jnp.where(zh == h, block, 0.0)
    t_copies = []
    for d in range(1, 4):
        to = lax.rem(x + d, 4)
        t_copies.append(send(tx.at[x, to], tx.at[x, to], x_peer(d)))
    far = send(tz.at[1 - zh], tzr, z_far)
    for copy in t_copies:
        copy.wait_recv()
    blocks = jnp.concatenate([tx[i, x] for i in range(4)], axis=0)
    high = blocks.astype(BF16)
    rest = blocks - high.astype(F32)
    middle = rest.astype(BF16)
    low = (rest - middle.astype(F32)).astype(BF16)
    contrib = jnp.zeros((512, 128), F32)
    for piece in (low, middle, high):
        contrib = contrib + lax.dot_general(p_mat[...], piece, (((0,), (0,)), ((), ())), preferred_element_type=F32)
    half[...] = contrib.reshape(2, 256, 128)
    swap = send(half.at[1 - c], half_r, sibling)

    swap.wait_recv()
    slab[...] = (half[c] + half_r[...]).reshape(8, 32, 128)
    s_copies = [None] * 8
    for d in (4, 3, 5, 2, 6, 1, 7):
        s_copies[d] = send(slab.at[lax.rem(y + d, 8)], slab_r.at[d - 1], y_peer(d))
    load_inv.wait()
    far.wait_recv()
    adjoint = jnp.concatenate([tz[zh, i] + tzr[i] for i in range(4)], axis=1) + inc_ref[...]
    grad_ref[...] = jnp.dot(adjoint, inv[...], precision=lax.Precision.HIGHEST, preferred_element_type=F32)
    total = slab[y]
    for d in (1, 7, 2, 6, 3, 5, 4):
        s_copies[d].wait_recv()
        total = total + slab_r[d - 1]
    zsum[z] = total
    s_copies = [send(zsum.at[z], zsum.at[z], z_peer(d)) for d in (4, 3, 5, 2, 6, 1, 7)]
    for copy in s_copies:
        copy.wait_recv()
    coded[c, x, y] = encode(jnp.sum(zsum[...], axis=0))

    def spread(source, d):
        piece = coded.at[c, x, source]
        for e in (2, 1, 3):
            x_copies[d, e] = send(piece, piece, x_peer(e))

    piece = coded.at[c, x, y]
    s_copies = [(d, send(piece, piece, y_peer(d))) for d in (4, 3, 5, 2, 6, 1, 7)]
    spread(y, 0)
    for d, copy in reversed(s_copies):
        copy.wait_recv()
        spread(lax.rem(y - d + 8, 8), d)
    last = [send(coded.at[c, x], coded.at[c, x], sibling)]
    for e in (1, 3, 2):
        for d in (0, 7, 1, 6, 2, 5, 3, 4):
            x_copies[d, e].wait_recv()
        source = lax.rem(x - e + 4, 4)
        last.append(send(coded.at[c, source], coded.at[c, source], sibling))
    for copy in last:
        copy.wait_recv()
    for h in range(2):
        for i in range(4):
            for j in range(8):
                low = h * 256 + j * 32
                term_ref[low : low + 32, i * 128 : i * 128 + 128] = decode(coded[h, i, j])
    line[1].wait_send()
    line[3].wait_send()
    for copy in copies:
        if copy is not None:
            copy.wait_send()


def on_device(adjoint_slab, panel_cols, incoming, inverse_block, panel_rows):
    vmem, hbm = pl.BlockSpec(memory_space=pltpu.VMEM), pl.BlockSpec(memory_space=pltpu.HBM)
    operands = (adjoint_slab, panel_cols.T, incoming, inverse_block, panel_rows)
    return pl.pallas_call(
        kernel,
        name="panel",
        out_shape=(
            pltpu.VMEM((24, 512), F32),
            pltpu.VMEM((512, 512), F32),
        ),
        in_specs=[hbm] * 5,
        out_specs=(vmem, vmem),
        scratch_shapes=[
            pltpu.VMEM((1536, 1024), BF16),
            pltpu.VMEM((512, 512), F32),
            pltpu.VMEM((24, 512), F32),
            pltpu.VMEM((24, 512), BF16),
            pltpu.VMEM((4, 128, 1024), BF16),
            pltpu.VMEM((4, 4, 8, 48, 128), F32),
            pltpu.VMEM((4, 2, 3, 208, 128), BF16),
            pltpu.VMEM((4, 2, 3, 208, 128), BF16),
            pltpu.VMEM((4, 7, 64, 128), BF16),
            pltpu.VMEM((4, 7, 64, 128), BF16),
            pltpu.VMEM((4, 48, 128), F32),
            pltpu.VMEM((2, 4, 24, 128), F32),
            pltpu.VMEM((4, 24, 128), F32),
            pltpu.VMEM((4, 4, 48, 128), F32),
            pltpu.VMEM((4, 2, 48, 256), BF16),
            pltpu.VMEM((192, 512), BF16),
            pltpu.VMEM((2, 256, 128), F32),
            pltpu.VMEM((256, 128), F32),
            pltpu.VMEM((8, 32, 128), F32),
            pltpu.VMEM((7, 32, 128), F32),
            pltpu.VMEM((8, 32, 128), F32),
            pltpu.VMEM((2, 4, 8, 48, 128), BF16),
            pltpu.SemaphoreType.DMA((5,)),
            pltpu.SemaphoreType.DMA((COPIES,)),
            pltpu.SemaphoreType.DMA((COPIES,)),
        ],
        compiler_params=pltpu.CompilerParams(
            collective_id=0, has_side_effects=True, vmem_limit_bytes=40 << 20
        ),
        cost_estimate=pl.CostEstimate(flops=2 << 30, bytes_accessed=8 << 20, transcendentals=1 << 20),
    )(*(pltpu.with_memory_space_constraint(array, pltpu.HBM) for array in operands))

def solution(mesh):
    return jax.shard_map(
        on_device,
        mesh=mesh,
        in_specs=(
            P("row", ("col", "depth")),
            P(("col", "depth"), "row"),
            P(("row", "col", "depth"), None),
            P(),
            P(("row", "col", "depth"), None),
        ),
        out_specs=(P(("row", "col", "depth"), None), P()),
        check_vma=False,
    )
```

```python
import jax
import jax.numpy as jnp
from jax import lax
from jax.experimental import pallas as pl
from jax.experimental.pallas import tpu as pltpu
from jax.sharding import PartitionSpec as P

MESH = pl.DeviceIdType.MESH
F32, BF16 = jnp.float32, jnp.bfloat16
STEPS = 250.0
HALF = 125.0
COPIES = 128
FAR = (4, 3, 5, 2)
NEAR = (6, 1, 7, 0)


def encode(value):
    groups = value.reshape(-1, 8, 128)
    size = jnp.abs(groups)
    scale = jnp.maximum(jnp.max(size, axis=0) * 1.004, 1e-30).astype(BF16)
    power = jnp.exp2(size * (STEPS / scale.astype(F32)) - HALF)
    code = jnp.where(groups < 0.0, -power, power).reshape(value.shape)
    scale = scale.astype(F32)
    return jnp.concatenate([code, scale, scale], axis=0).astype(BF16)


def decode(coded):
    coded = coded.astype(F32)
    rows = coded.shape[0] - 16
    groups = coded[:rows].reshape(-1, 8, 128)
    scale = coded[rows : rows + 8] * (1.0 / STEPS)
    steps = jnp.log2(jnp.abs(groups)) + HALF
    return (jnp.where(groups < 0.0, -steps, steps) * scale).reshape(rows, 128)


def kernel(
    a_hbm, b_hbm, inc_hbm, inv_hbm, p_hbm,
    grad_ref, term_ref,
    a, inv, inc_ref, p_ref, b_all, own, xs, xr, ys, yr, yown, tz, tzr, tx, p_all, p_mat,
    half, half_r, slab, slab_r, zsum, coded, local_sem, send_sem, recv_sem,
):
    row, col, x = lax.axis_index("row"), lax.axis_index("col"), lax.axis_index("depth")
    zl, c = lax.div(row, 2), lax.rem(row, 2)
    y, zh = lax.div(col, 2), lax.rem(col, 2)
    z = zh * 4 + zl

    def at(x=x, y=y, zh=zh, zl=zl, c=c):
        return (zl * 2 + c, y * 2 + zh, x)

    def x_peer(d):
        return at(x=lax.rem(x + d, 4))

    def y_peer(d):
        return at(y=lax.rem(y + d, 8))

    def z_peer(d):
        other = lax.rem(z + d, 8)
        return at(zh=lax.div(other, 4), zl=lax.rem(other, 4))

    sibling = at(c=1 - c)
    z_far = at(zh=1 - zh)

    mine = pl.ds(pl.multiple_of(c * 64, 64), 64)
    loads = []
    for i, (src, dst) in enumerate((
        (p_hbm, p_ref), (b_hbm, b_all.at[zl, mine]), (a_hbm, a), (inc_hbm, inc_ref), (inv_hbm, inv),
    )):
        loads.append(pltpu.make_async_copy(src, dst, local_sem.at[i]))
        loads[-1].start()
    load_p, load_b, load_a, load_inc, load_inv = loads

    barrier = pltpu.get_barrier_semaphore()
    peers = [sibling] + [x_peer(d) for d in range(1, 4)]
    peers += [y_peer(d) for d in range(1, 8)] + [z_peer(d) for d in range(1, 8)]
    for peer in peers:
        pl.semaphore_signal(barrier, inc=1, device_id=peer, device_id_type=MESH)

    pl.semaphore_wait(barrier, len(peers))

    copies = []

    def plan(src, dst, target, send_index=None, recv_index=None):
        i = len(copies)
        copies.append(None)
        return pltpu.make_async_remote_copy(
            src_ref=src, dst_ref=dst,
            send_sem=send_sem.at[i if send_index is None else send_index],
            recv_sem=recv_sem.at[i if recv_index is None else recv_index],
            device_id=target, device_id_type=MESH,
        )

    def send(src, dst, target):
        copy = plan(src, dst, target)
        copy.start()
        copies[-1] = copy
        return copy

    middle = lax.div(lax.rem(zl, 3) + 1, 2)
    two, three = lax.rem(zl + 2, 4), 3 - zl
    chunk = [
        zl,
        zl + 1 - 2 * lax.rem(zl, 2),
        middle * three + (1 - middle) * two,
        middle * two + (1 - middle) * three,
    ]
    slots = [None, 0, 1 + middle, 2 - middle]
    sib = send(b_hbm, b_all.at[zl, mine], sibling)
    first = len(copies)
    line = [None] + [
        plan(b_hbm, b_all.at[zl, mine], at(zl=chunk[k]), first + k - 1, first + slots[k]) for k in range(1, 4)
    ]
    line[1].start()

    @pl.when(middle == 1)
    def _():
        line[2].start()

    load_p.wait()
    wide = jnp.concatenate([p_ref[:, :256].astype(F32), p_ref[:, 256:].astype(F32)], axis=0)
    p_all[x, zh] = wide.astype(BF16)
    p_far = send(p_all.at[x, zh], p_all.at[x, zh], z_far)
    p_copies = [send(p_all.at[x, zh], p_all.at[x, zh], x_peer(d)) for d in range(1, 4)]
    load_a.wait()
    load_b.wait()
    sib.wait_recv()
    x_copies = {}
    y_copies = {}

    def multiply(k):
        for part in range(2):
            acc = lax.dot_general(
                a[part * 768 : part * 768 + 768, :], b_all[chunk[k]], (((1,), (1,)), ((), ())), preferred_element_type=F32
            )
            for yy in range(4):
                for to in range(4):
                    low = yy * 192 + to * 24
                    own[k, to, part * 4 + yy, :24, :] = acc[low : low + 24]
                    own[k, to, part * 4 + yy, 24:, :] = acc[low + 96 : low + 120]
        for part, order in enumerate((FAR, NEAR)):
            for d in (2, 1, 3):
                xs[k, part, d - 1] = encode(blocks_of(k, lax.rem(x + d, 4), order))
                x_copies[k, part, d] = send(xs.at[k, part, d - 1], xr.at[k, part, d - 1], x_peer(d))

    def blocks_of(k, to, order):
        return jnp.concatenate([own[k, to, lax.rem(y + e, 8)] for e in order], axis=0)

    def reduce_x(k, part):
        order = (FAR, NEAR)[part]
        total = blocks_of(k, x, order)
        for d in (1, 3, 2):
            x_copies[k, part, d].wait_recv()
            total = total + decode(xr[k, part, d - 1])
        for j, d in enumerate(order):
            block = total[j * 48 : j * 48 + 48]
            if d == 0:
                yown[k] = block
            else:
                ys[k, d - 1] = encode(block)
                y_copies[k, d] = send(ys.at[k, d - 1], yr.at[k, d - 1], y_peer(d))

    def reduce_y(k):
        total = yown[k]
        for d in (4, 3, 5, 2, 6, 1, 7):
            y_copies[k, d].wait_recv()
            total = total + decode(yr[k, d - 1])
        for h in range(2):
            tz[h, chunk[k]] = total[h * 24 : h * 24 + 24] * -2.0

    multiply(0)

    @pl.when(middle == 1)
    def _():
        line[2].wait_send()
        line[3].start()

    def arrive(k):
        line[k].wait_recv()
        there = b_all.at[chunk[k], mine]
        return send(there, there, sibling)

    forward = arrive(1)
    p_far.wait_recv()
    p_copies += [send(p_all.at[x, 1 - zh], p_all.at[x, 1 - zh], x_peer(d)) for d in range(1, 4)]

    @pl.when(middle == 0)
    def _():
        line[2].start()

    forward.wait_recv()
    multiply(1)

    @pl.when(middle == 0)
    def _():
        line[2].wait_send()
        line[3].start()

    forward = arrive(2)
    reduce_x(0, 0)
    reduce_x(0, 1)
    forward.wait_recv()
    multiply(2)
    forward = arrive(3)
    forward.wait_recv()
    multiply(3)
    reduce_x(1, 0)
    reduce_x(1, 1)
    reduce_x(2, 0)
    reduce_x(2, 1)
    reduce_x(3, 0)
    reduce_x(3, 1)
    for copy in p_copies:
        copy.wait_recv()
    for i in range(4):
        both = p_all[i].astype(F32)
        rows = [jnp.concatenate([both[h, :24], both[h, 24:]], axis=1) for h in range(2)]
        p_mat[i * 48 : i * 48 + 48, :] = jnp.concatenate(rows, axis=0).astype(BF16)
    reduce_y(0)
    reduce_y(1)
    reduce_y(2)
    reduce_y(3)

    load_inc.wait()
    for i in range(4):
        block = inc_ref[:, i * 128 : i * 128 + 128]
        for h in range(2):
            tx[x, i, h * 24 : h * 24 + 24, :] = tz[h, i] + jnp.where(zh == h, block, 0.0)
    t_copies = []
    for d in range(1, 4):
        to = lax.rem(x + d, 4)
        t_copies.append(send(tx.at[x, to], tx.at[x, to], x_peer(d)))
    far = send(tz.at[1 - zh], tzr, z_far)
    for copy in t_copies:
        copy.wait_recv()
    blocks = jnp.concatenate([tx[i, x] for i in range(4)], axis=0)
    high = blocks.astype(BF16)
    rest = blocks - high.astype(F32)
    middle = rest.astype(BF16)
    low = (rest - middle.astype(F32)).astype(BF16)
    contrib = jnp.zeros((512, 128), F32)
    for piece in (low, middle, high):
        contrib = contrib + lax.dot_general(p_mat[...], piece, (((0,), (0,)), ((), ())), preferred_element_type=F32)
    half[...] = contrib.reshape(2, 256, 128)
    swap = send(half.at[1 - c], half_r, sibling)

    swap.wait_recv()
    slab[...] = (half[c] + half_r[...]).reshape(8, 32, 128)
    s_copies = [None] * 8
    for d in (4, 3, 5, 2, 6, 1, 7):
        s_copies[d] = send(slab.at[lax.rem(y + d, 8)], slab_r.at[d - 1], y_peer(d))
    load_inv.wait()
    far.wait_recv()
    adjoint = jnp.concatenate([tz[zh, i] + tzr[i] for i in range(4)], axis=1) + inc_ref[...]
    grad_ref[...] = jnp.dot(adjoint, inv[...], precision=lax.Precision.HIGHEST, preferred_element_type=F32)
    total = slab[y]
    for d in (1, 7, 2, 6, 3, 5, 4):
        s_copies[d].wait_recv()
        total = total + slab_r[d - 1]
    zsum[z] = total
    s_copies = [send(zsum.at[z], zsum.at[z], z_peer(d)) for d in (4, 3, 5, 2, 6, 1, 7)]
    for copy in s_copies:
        copy.wait_recv()
    coded[c, x, y] = encode(jnp.sum(zsum[...], axis=0))

    def spread(source, d):
        piece = coded.at[c, x, source]
        for e in (2, 1, 3):
            x_copies[d, e] = send(piece, piece, x_peer(e))

    piece = coded.at[c, x, y]
    s_copies = [(d, send(piece, piece, y_peer(d))) for d in (4, 3, 5, 2, 6, 1, 7)]
    spread(y, 0)
    for d, copy in reversed(s_copies):
        copy.wait_recv()
        spread(lax.rem(y - d + 8, 8), d)
    last = [send(coded.at[c, x], coded.at[c, x], sibling)]
    for e in (1, 3, 2):
        for d in (0, 7, 1, 6, 2, 5, 3, 4):
            x_copies[d, e].wait_recv()
        source = lax.rem(x - e + 4, 4)
        last.append(send(coded.at[c, source], coded.at[c, source], sibling))
    for copy in last:
        copy.wait_recv()
    for h in range(2):
        for i in range(4):
            for j in range(8):
                low = h * 256 + j * 32
                term_ref[low : low + 32, i * 128 : i * 128 + 128] = decode(coded[h, i, j])
    line[1].wait_send()
    line[3].wait_send()
    for copy in copies:
        if copy is not None:
            copy.wait_send()


def on_device(adjoint_slab, panel_cols, incoming, inverse_block, panel_rows):
    vmem, hbm = pl.BlockSpec(memory_space=pltpu.VMEM), pl.BlockSpec(memory_space=pltpu.HBM)
    operands = (adjoint_slab, panel_cols.T, incoming, inverse_block, panel_rows)
    return pl.pallas_call(
        kernel,
        name="panel",
        out_shape=(
            pltpu.VMEM((24, 512), F32),
            pltpu.VMEM((512, 512), F32),
        ),
        in_specs=[hbm] * 5,
        out_specs=(vmem, vmem),
        scratch_shapes=[
            pltpu.VMEM((1536, 1024), BF16),
            pltpu.VMEM((512, 512), F32),
            pltpu.VMEM((24, 512), F32),
            pltpu.VMEM((24, 512), BF16),
            pltpu.VMEM((4, 128, 1024), BF16),
            pltpu.VMEM((4, 4, 8, 48, 128), F32),
            pltpu.VMEM((4, 2, 3, 208, 128), BF16),
            pltpu.VMEM((4, 2, 3, 208, 128), BF16),
            pltpu.VMEM((4, 7, 64, 128), BF16),
            pltpu.VMEM((4, 7, 64, 128), BF16),
            pltpu.VMEM((4, 48, 128), F32),
            pltpu.VMEM((2, 4, 24, 128), F32),
            pltpu.VMEM((4, 24, 128), F32),
            pltpu.VMEM((4, 4, 48, 128), F32),
            pltpu.VMEM((4, 2, 48, 256), BF16),
            pltpu.VMEM((192, 512), BF16),
            pltpu.VMEM((2, 256, 128), F32),
            pltpu.VMEM((256, 128), F32),
            pltpu.VMEM((8, 32, 128), F32),
            pltpu.VMEM((7, 32, 128), F32),
            pltpu.VMEM((8, 32, 128), F32),
            pltpu.VMEM((2, 4, 8, 48, 128), BF16),
            pltpu.SemaphoreType.DMA((5,)),
            pltpu.SemaphoreType.DMA((COPIES,)),
            pltpu.SemaphoreType.DMA((COPIES,)),
        ],
        compiler_params=pltpu.CompilerParams(
            collective_id=0, has_side_effects=True, vmem_limit_bytes=40 << 20
        ),
        cost_estimate=pl.CostEstimate(flops=2 << 30, bytes_accessed=8 << 20, transcendentals=1 << 20),
    )(*(pltpu.with_memory_space_constraint(array, pltpu.HBM) for array in operands))

def solution(mesh):
    return jax.shard_map(
        on_device,
        mesh=mesh,
        in_specs=(
            P("row", ("col", "depth")),
            P(("col", "depth"), "row"),
            P(("row", "col", "depth"), None),
            P(),
            P(("row", "col", "depth"), None),
        ),
        out_specs=(P(("row", "col", "depth"), None), P()),
        check_vma=False,
    )
```
